128 devices in a mesh: pipe: 2 (over x_lo), seq: 32 (over z, y, x_hi), tp: 2 (over core).
Axes of the slice: x: 4 (x_hi: 2, x_lo: 2; x = x_hi * 2 + x_lo), y: 4, z: 4, core: 2. Of those that a mesh axis runs over, the one named last changes fastest.
Arguments:
- queries: bfloat16 [14336, 4096], P(('pipe', 'seq', 'tp')), may hold values from -45 to 45
- keys: bfloat16 [14336, 4096], P(('pipe', 'seq', 'tp')), may hold values from -8 to 8
- values: bfloat16 [14336, 4096], P(('pipe', 'seq', 'tp')), may hold values from -6 to 6
- stale_keys: bfloat16 [14336, 4096], P(('pipe', 'seq', 'tp')), may hold values from -8 to 8
- stale_values: bfloat16 [14336, 4096], P(('pipe', 'seq', 'tp')), may hold values from -6 to 6
- group_order: int32 [2, 4], replicated, may hold values from 0 to 3, each once within a row
Outputs:
- attended: bfloat16 [14336, 4096], P(('pipe', 'seq', 'tp'))
The draws below stay inside these ranges and needn't reach their ends.
All inputs are finite; a program needn't handle non-finite values.
Results may differ from the reference program's by a relative error of at most 0.025.
Values may be sent and summed in bfloat16 or wider, within the bound.
A program may use at most 128 MiB of HBM per device.

```python
import math
import jax
import jax.numpy as jnp
from jax import lax

HD = 128
HEADS = 32
GPS = 4
TOKENS = 14336
GROUP_TOK = 1792
N_PIPE = 2


def draw_queries(key, part):
    key = jax.random.fold_in(key, 11)
    drawn = jax.random.truncated_normal(key, -4.0, 4.0, (TOKENS, HEADS * HD), jnp.float32)
    return drawn.astype(jnp.bfloat16)


def keyed_rows(key):
    drawn = jax.random.truncated_normal(key, -4.0, 4.0, (TOKENS, HEADS * HD), jnp.float32)
    return drawn.astype(jnp.bfloat16)


def draw_keys(key, part):
    key = jax.random.fold_in(key, 23)
    return keyed_rows(key)


def draw_stale_keys(key, part):
    key = jax.random.fold_in(key, 37)
    return keyed_rows(key)


def block_levels(stream_key, dims, pieces, low, largest):
    gain = 1.0
    for position, shards_of in pieces:
        steps = jax.random.uniform(jax.random.fold_in(jax.random.fold_in(stream_key, 6), position), (shards_of,), jnp.float32, low / len(pieces), largest / len(pieces))
        gain = gain * jnp.repeat(jnp.exp(steps), dims[position] // shards_of).reshape((-1,) + (1,) * (len(dims) - 1 - position))
    return gain


def bell_draw(stream_key, dims, width, reach, cuts=(), kind=jnp.bfloat16):
    array = width * jax.random.normal(stream_key, dims, jnp.float32)
    if cuts:
        array = array * block_levels(stream_key, dims, cuts, -0.22, 0.18)
    return jnp.clip(array, -reach, reach).astype(kind)


def setup_inputs(seed: int = 0) -> dict:
    key_of = jax.random.split(jax.random.key(seed), 7)
    return {
        "queries": draw_queries(jax.random.fold_in(key_of[6], 71), 0),
        "keys": draw_keys(jax.random.fold_in(key_of[6], 71), 0),
        "values": bell_draw(key_of[2], (TOKENS, HEADS * HD), 1.0, 6.0, ((0, 128),)),
        "stale_keys": draw_stale_keys(jax.random.fold_in(key_of[6], 71), 0),
        "stale_values": bell_draw(key_of[4], (TOKENS, HEADS * HD), 1.0, 6.0, ((0, 128),)),
        "group_order": jax.vmap(lambda own: jax.random.permutation(own, GPS))(jax.random.split(key_of[5], N_PIPE)).reshape((N_PIPE, GPS)).astype(jnp.int32),
    }


def group_times(group_order):
    sections, groups = group_order.shape
    match = group_order[:, :, None] == jnp.arange(groups, dtype=jnp.int32)[None, None, :]
    turns = lax.optimization_barrier(jnp.sum(jnp.arange(groups, dtype=jnp.int32)[None, :, None] * match.astype(jnp.int32), axis=1))
    return (turns + jnp.arange(sections, dtype=jnp.int32)[:, None]).reshape(sections * groups)

def reference(queries, keys, values, stale_keys, stale_values, group_order):
    timing = group_times(group_order)
    group_count = N_PIPE * GPS
    key_group = jnp.arange(TOKENS, dtype=jnp.int32) // GROUP_TOK
    key_time = timing[key_group]
    scaling = 1.0 / math.sqrt(HD)

    def one_head(head):
        first = head * HD
        head_query = lax.dynamic_slice_in_dim(queries, first, HD, 1).astype(jnp.float32)
        head_keys = lax.dynamic_slice_in_dim(keys, first, HD, 1).astype(jnp.float32)
        head_values = lax.dynamic_slice_in_dim(values, first, HD, 1).astype(jnp.float32)
        old_keys = lax.dynamic_slice_in_dim(stale_keys, first, HD, 1).astype(jnp.float32)
        old_values = lax.dynamic_slice_in_dim(stale_values, first, HD, 1).astype(jnp.float32)

        def one_group(group):
            block = lax.dynamic_slice_in_dim(head_query, group * GROUP_TOK, GROUP_TOK, 0)
            own_time = timing[group]
            fresh = (key_time < own_time) | (key_group == group)
            chosen_keys = jnp.where(fresh[:, None], head_keys, old_keys)
            chosen_values = jnp.where(fresh[:, None], head_values, old_values)
            scores = jnp.dot(block, chosen_keys.T, precision=lax.Precision.HIGHEST) * scaling
            peak = lax.optimization_barrier(jnp.max(scores, axis=1, keepdims=True))
            weights = jnp.exp(scores - peak)
            total = lax.optimization_barrier(jnp.sum(weights, axis=1))
            rounded = lax.optimization_barrier(weights.astype(jnp.bfloat16)).astype(jnp.float32)
            mixed = jnp.dot(rounded, chosen_values, precision=lax.Precision.HIGHEST) / total[:, None]
            return mixed.astype(jnp.bfloat16)
        return lax.map(one_group, jnp.arange(group_count, dtype=jnp.int32))
    stacked = lax.map(one_head, jnp.arange(HEADS, dtype=jnp.int32))
    return jnp.transpose(stacked, (1, 2, 0, 3)).reshape(TOKENS, HEADS * HD)
```

```python
import functools
import math

import jax
import jax.numpy as jnp
from jax import lax
from jax.experimental import pallas as pl
from jax.experimental.pallas import tpu as pltpu
from jax.sharding import PartitionSpec as P

MESH = pl.DeviceIdType.MESH
GPS = 4
HD = 128
NZ, NY, NX = 4, 4, 2
SLOTS = NZ * NX
CHUNKS = NY
START = -1e30


def freshness(group_order):
    sections, groups = group_order.shape
    match = group_order[:, :, None] == jnp.arange(groups, dtype=jnp.int32)[None, None, :]
    turns = jnp.sum(
        jnp.arange(groups, dtype=jnp.int32)[None, :, None] * match.astype(jnp.int32), axis=1
    )
    times = (turns + jnp.arange(sections, dtype=jnp.int32)[:, None]).reshape(sections * groups)
    own = jnp.eye(sections * groups, dtype=jnp.bool_)
    return ((times[None, :] < times[:, None]) | own).astype(jnp.int32)


def kernel(
    fresh_ref, q_ref, k_ref, v_ref, sk_ref, sv_ref, out_ref,
    q_buf, kv_buf, acc, peak, part_out, part_in, lse_out, lse_in, done_buf,
    local_sem, q_send, q_recv, qf_send, qf_recv, kv_send, kv_recv, fwd_send, fwd_recv,
    part_send, part_recv, lse_send, lse_recv, done_send, done_recv,
):
    pipe, seq, tp = lax.axis_index("pipe"), lax.axis_index("seq"), lax.axis_index("tp")
    z, y, x = seq // (NY * NX), (seq // NX) % NY, seq % NX
    rows = q_ref.shape[0]
    block = NY * rows
    chunk_keys = 2 * SLOTS * rows
    scaling = math.log2(math.e) / math.sqrt(HD)
    sibling = {"tp": 1 - tp}
    across = {"pipe": 1 - pipe}

    def partner(dz, dy, dx):
        other = (((z + dz) % NZ) * NY + (y + dy) % NY) * NX + (x + dx) % NX
        return other, {"seq": other, "pipe": (pipe + dx) % 2}

    def offset(chunk, slot):
        dz, dx = slot % NZ, slot // NZ
        return dz, (dz + chunk) % NY, dx

    def remote(src, dst, send, recv, device):
        return pltpu.make_async_remote_copy(
            src_ref=src, dst_ref=dst, send_sem=send, recv_sem=recv,
            device_id=device, device_id_type=MESH,
        )

    def bytes_of(view, sem):
        pltpu.make_async_copy(view, view, sem).wait()

    barrier = pltpu.get_barrier_semaphore()

    def greet(index, _):
        _, device = partner(*offset(index // SLOTS, index % SLOTS))
        pl.semaphore_signal(barrier, inc=1, device_id=device, device_id_type=MESH)
        return 0

    lax.fori_loop(1, CHUNKS * SLOTS, greet, 0)
    pl.semaphore_signal(barrier, inc=1, device_id=sibling, device_id_type=MESH)
    pl.semaphore_signal(barrier, inc=1, device_id=across, device_id_type=MESH)
    pl.semaphore_wait(barrier, CHUNKS * SLOTS + 1)

    def head(ref, which):
        return ref.at[:, pl.ds(pl.multiple_of(which * HD, HD), HD)]

    def kv_refs():
        return ((k_ref, 0, 0), (sk_ref, 0, 1), (v_ref, 1, 0), (sv_ref, 1, 1))

    def send_queries(index, _):
        dz, dy, dx = offset(index // SLOTS, index % SLOTS)
        other, device = partner(dz, dy, dx)
        remote(head(q_ref, other), q_buf.at[0, dx, z, y], q_send, q_recv, device).start()
        return 0

    lax.fori_loop(1, CHUNKS * SLOTS, send_queries, 0)
    own_q = pltpu.make_async_copy(head(q_ref, seq), q_buf.at[0, 0, z, y], local_sem.at[0])
    own_q.start()

    def send_kv(index, _):
        chunk, slot = index // SLOTS, index % SLOTS
        other, device = partner(*offset(chunk, slot))
        for ref, kind, version in kv_refs():
            remote(
                head(ref, other), kv_buf.at[chunk, tp, slot, kind, version],
                kv_send.at[chunk], kv_recv.at[chunk], device,
            ).start()
        return 0

    lax.fori_loop(1, CHUNKS * SLOTS, send_kv, 0)
    own_kv = []
    for number, (ref, kind, version) in enumerate(kv_refs()):
        copy = pltpu.make_async_copy(
            head(ref, seq), kv_buf.at[0, tp, 0, kind, version], local_sem.at[1 + number]
        )
        copy.start()
        own_kv.append(copy)

    def clear(index, _):
        acc[index] = jnp.zeros(acc.shape[1:], jnp.float32)
        peak[index] = jnp.full(peak.shape[1:], START, jnp.float32)
        return 0

    lax.fori_loop(0, 4 * NZ, clear, 0)

    def others(ref):
        return ref.at[0, pl.ds(0, 7)]

    def forward_q():
        return remote(q_buf.at[0], q_buf.at[1], qf_send, qf_recv, across)

    def forward_kv(chunk):
        mine = kv_buf.at[chunk, tp]
        return remote(mine, mine, fwd_send.at[chunk], fwd_recv.at[chunk], sibling)

    def other_blocks(count_view, sem):
        bytes_of(count_view, sem)

    arrived = out_ref.at[:, pl.ds(0, (CHUNKS * SLOTS - 1) * HD)]
    bytes_of(arrived, q_recv)
    own_q.wait()
    forward_q().start()
    bytes_of(kv_buf.at[0, tp, pl.ds(1, SLOTS - 1)], kv_recv.at[0])
    for copy in own_kv:
        copy.wait()
    forward_kv(0).start()
    forward_kv(0).wait_recv()

    ones = jnp.ones((chunk_keys, HD), jnp.bfloat16)

    def chosen(chunk, kind, query_group):
        pieces = []
        for slot in range(SLOTS):
            key_group = ((pipe + slot // NZ) % 2) * GPS + (z + NZ - slot % NZ) % NZ
            fresh = fresh_ref[query_group, key_group] != 0
            for core in range(2):
                pieces.append(
                    jnp.where(
                        fresh,
                        kv_buf[chunk, core, slot, kind, 0],
                        kv_buf[chunk, core, slot, kind, 1],
                    )
                )
        return jnp.concatenate(pieces, axis=0)

    def attend(chunk, half, dx):
        first = (half * NX + dx) * NZ
        query_pipe = (pipe + dx + half) % 2

        def score(number):
            queries = q_buf[half, dx, number].reshape(block, HD)
            keys = chosen(chunk, 0, query_pipe * GPS + number)
            return lax.dot_general(
                queries, keys, (((1,), (1,)), ((), ())), preferred_element_type=jnp.float32
            )

        scores = score(0)
        for number in range(NZ):
            later = score(number + 1) if number + 1 < NZ else None
            values = chosen(chunk, 1, query_pipe * GPS + number)
            values = jnp.concatenate([values, ones], axis=1)
            before = peak[first + number, :, :1]
            now = jnp.maximum(before, jnp.max(scores, axis=1, keepdims=True) * scaling)
            weights = jnp.exp2(scores * scaling - now).astype(jnp.bfloat16)
            factor = jnp.exp2(before - now)
            acc[first + number] = acc[first + number] * factor + jnp.dot(
                weights, values, preferred_element_type=jnp.float32
            )
            peak[first + number] = jnp.broadcast_to(now, (block, HD))
            scores = later

    def finished(index):
        total = acc[index, :, HD : HD + 1]
        level = peak[index, :, :1] + jnp.log2(total)
        return acc[index, :, :HD] / total, level

    def exchange(dx):
        return (
            remote(part_out.at[dx], part_in.at[dx], part_send.at[dx], part_recv.at[dx], across),
            remote(lse_out.at[dx], lse_in.at[dx], lse_send.at[dx], lse_recv.at[dx], across),
        )

    def hand_over(dx):
        for number in range(NZ):
            mixed, level = finished((NX + dx) * NZ + number)
            part_out[dx, number] = mixed.astype(jnp.bfloat16)
            wide = jnp.concatenate(
                [
                    jnp.broadcast_to(level, (block, HD)),
                    jnp.zeros((lse_out.shape[3] - block, HD), jnp.float32),
                ],
                axis=0,
            )
            lse_out[dx, number] = jnp.transpose(wide)[:8]
        for copy in exchange(dx):
            copy.start()

    def give_back(dx):
        for copy in exchange(dx):
            copy.wait_recv()
        for number in range(NZ):
            mine, level = finished(dx * NZ + number)
            wide = jnp.concatenate(
                [lse_in[dx, number]] * (HD // 8), axis=0
            )
            other_level = jnp.transpose(wide)[:block, :1]
            top = jnp.maximum(level, other_level)
            share, other_share = jnp.exp2(level - top), jnp.exp2(other_level - top)
            both = 1.0 / (share + other_share)
            mixed = mine * (share * both) + part_in[dx, number].astype(jnp.float32) * (
                other_share * both
            )
            done_buf[dx, number] = mixed.astype(jnp.bfloat16).reshape(NY, rows, HD)

        def send_back(index, _):
            back_z, back_y = index // NY, index % NY
            other = (back_z * NY + back_y) * NX + (x + dx) % NX
            target = {"seq": other, "pipe": (pipe + dx) % 2}

            @pl.when(jnp.logical_or(other != seq, dx != 0))
            def _():
                remote(
                    done_buf.at[dx, back_z, back_y], head(out_ref, seq),
                    done_send, done_recv, target,
                ).start()

            return 0

        lax.fori_loop(0, NZ * NY, send_back, 0)

    def step(index, _):
        chunk, turn = index // 4, index % 4
        dx = turn % 2
        half = jnp.where(chunk == 0, turn // 2, 1 - turn // 2)

        @pl.when(index == 2)
        def _():
            forward_q().wait_recv()

        @pl.when(jnp.logical_and(turn == 0, chunk > 0))
        def _():
            forward_kv(chunk).wait_recv()

        @pl.when(jnp.logical_and(turn == 2, chunk < CHUNKS - 1))
        def _():
            bytes_of(kv_buf.at[chunk + 1, tp], kv_recv.at[chunk + 1])
            forward_kv(chunk + 1).start()

        attend(chunk, half, dx)

        @pl.when(jnp.logical_and(chunk == CHUNKS - 1, turn < 2))
        def _():
            hand_over(dx)

        @pl.when(jnp.logical_and(chunk == CHUNKS - 1, turn >= 2))
        def _():
            give_back(dx)

        return 0

    lax.fori_loop(0, 4 * CHUNKS, step, 0)

    own_out = pltpu.make_async_copy(done_buf.at[0, z, y], head(out_ref, seq), local_sem.at[5])
    own_out.start()
    own_out.wait()
    bytes_of(arrived, q_send)
    forward_q().wait_send()
    bytes_of(kv_buf.at[0, tp, pl.ds(1, SLOTS - 1)], kv_send.at[0])
    for chunk in range(1, CHUNKS):
        bytes_of(kv_buf.at[chunk, tp], kv_send.at[chunk])
    for chunk in range(CHUNKS):
        forward_kv(chunk).wait_send()
    for dx in range(NX):
        for copy in exchange(dx):
            copy.wait_send()
    bytes_of(arrived, done_send)
    bytes_of(arrived, done_recv)


def local(queries, keys, values, stale_keys, stale_values, group_order):
    rows, columns = queries.shape
    block = NY * rows
    dma = pltpu.SemaphoreType.DMA
    anywhere = pl.BlockSpec(memory_space=pl.ANY)
    return pl.pallas_call(
        kernel,
        out_shape=jax.ShapeDtypeStruct((rows, columns), jnp.bfloat16),
        in_specs=[pl.BlockSpec(memory_space=pltpu.SMEM)] + [anywhere] * 5,
        out_specs=anywhere,
        scratch_shapes=[
            pltpu.VMEM((2, NX, NZ, NY, rows, HD), jnp.bfloat16),
            pltpu.VMEM((CHUNKS, 2, SLOTS, 2, 2, rows, HD), jnp.bfloat16),
            pltpu.VMEM((2 * NX * NZ, block, 2 * HD), jnp.float32),
            pltpu.VMEM((2 * NX * NZ, block, HD), jnp.float32),
            pltpu.VMEM((NX, NZ, block, HD), jnp.bfloat16),
            pltpu.VMEM((NX, NZ, block, HD), jnp.bfloat16),
            pltpu.VMEM((NX, NZ, 8, 512), jnp.float32),
            pltpu.VMEM((NX, NZ, 8, 512), jnp.float32),
            pltpu.VMEM((NX, NZ, NY, rows, HD), jnp.bfloat16),
            dma((6,)), dma, dma, dma, dma,
            dma((CHUNKS,)), dma((CHUNKS,)), dma((CHUNKS,)), dma((CHUNKS,)),
            dma((NX,)), dma((NX,)), dma((NX,)), dma((NX,)), dma, dma,
        ],
        compiler_params=pltpu.CompilerParams(
            collective_id=0, has_side_effects=True, vmem_limit_bytes=60 * 2**20
        ),
    )(freshness(group_order), queries, keys, values, stale_keys, stale_values)


def solution(mesh):
    placed = P(("pipe", "seq", "tp"), None)
    return jax.shard_map(
        local, mesh=mesh, in_specs=(placed,) * 5 + (P(),), out_specs=placed, check_vma=False
    )
```

```python
import functools
import math

import jax
import jax.numpy as jnp
from jax import lax
from jax.experimental import pallas as pl
from jax.experimental.pallas import tpu as pltpu
from jax.sharding import PartitionSpec as P

MESH = pl.DeviceIdType.MESH
GPS = 4
HD = 128
NZ, NY, NX = 4, 4, 2
SLOTS = NZ * NX
CHUNKS = NY
START = -1e30


STEPS = (
    ((0, 0, 0), (0, 0, 1), (1, 0, 0), (3, 0, 0), (0, 1, 0), (0, 3, 0), (1, 1, 1), (3, 3, 0)),
    ((0, 2, 0), (3, 1, 1), (2, 0, 1), (3, 1, 0), (2, 3, 0), (1, 3, 1), (0, 1, 1), (1, 3, 0)),
    ((2, 0, 0), (0, 3, 1), (3, 2, 0), (0, 2, 1), (2, 1, 1), (1, 0, 1), (2, 2, 0), (2, 2, 1)),
    ((3, 3, 1), (2, 1, 0), (1, 1, 0), (2, 3, 1), (1, 2, 0), (3, 2, 1), (3, 0, 1), (1, 2, 1)),
)
ORDER = (
    (0, 0, 0), (0, 1, 0), (1, 0, 0), (0, 0, 1), (0, 1, 1), (1, 1, 0), (1, 0, 1), (1, 1, 1),
    (1, 0, 2), (1, 1, 2), (1, 0, 3), (1, 1, 3), (0, 0, 2), (0, 0, 3), (0, 1, 2), (0, 1, 3),
)


def lookup(index, table):
    found = table[0]
    for at in range(1, len(table)):
        if table[at] != table[at - 1]:
            found = jnp.where(index >= at, table[at], found)
    return found


def kernel(
    order_ref, q_ref, k_ref, v_ref, sk_ref, sv_ref, out_ref,
    q_buf, kv_buf, acc, peak, part_out, part_in, lse_out, lse_in, done_buf,
    time_ref, group_ref,
    local_sem, q_send, q_recv, qf_send, qf_recv, kv_send, kv_recv, fwd_send, fwd_recv,
    part_send, part_recv, lse_send, lse_recv, done_send, done_recv,
):
    pipe, seq, tp = lax.axis_index("pipe"), lax.axis_index("seq"), lax.axis_index("tp")
    z, y, x = seq // (NY * NX), (seq // NX) % NY, seq % NX
    rows = q_ref.shape[0]
    block = NY * rows
    chunk_keys = 2 * SLOTS * rows
    scaling = math.log2(math.e) / math.sqrt(HD)
    sibling = {"tp": 1 - tp}
    across = {"pipe": 1 - pipe}

    def partner(dz, dy, dx):
        other = (((z + dz) % NZ) * NY + (y + dy) % NY) * NX + (x + dx) % NX
        return other, {"seq": other, "pipe": (pipe + dx) % 2}

    def remote(src, dst, send, recv, device):
        return pltpu.make_async_remote_copy(
            src_ref=src, dst_ref=dst, send_sem=send, recv_sem=recv,
            device_id=device, device_id_type=MESH,
        )

    def bytes_of(view, sem):
        pltpu.make_async_copy(view, view, sem).wait()

    barrier = pltpu.get_barrier_semaphore()

    def greet(index, _):
        _, device = partner(index // (NY * NX), (index // NX) % NY, index % NX)
        pl.semaphore_signal(barrier, inc=1, device_id=device, device_id_type=MESH)
        return 0

    lax.fori_loop(1, CHUNKS * SLOTS, greet, 0)
    pl.semaphore_signal(barrier, inc=1, device_id=sibling, device_id_type=MESH)
    pl.semaphore_signal(barrier, inc=1, device_id=across, device_id_type=MESH)
    pl.semaphore_wait(barrier, CHUNKS * SLOTS + 1)

    def head(ref, which):
        return ref.at[:, pl.ds(pl.multiple_of(which * HD, HD), HD)]

    def kv_refs():
        return ((k_ref, 0, 0), (sk_ref, 0, 1), (v_ref, 1, 0), (sv_ref, 1, 1))

    def send_kv(chunk):
        for slot, step in enumerate(STEPS[chunk]):
            if step == (0, 0, 0):
                continue
            other, device = partner(*step)
            for ref, kind, version in kv_refs():
                remote(
                    head(ref, other), kv_buf.at[chunk, tp, slot, kind, version],
                    kv_send.at[chunk], kv_recv.at[chunk], device,
                ).start()

    def send_queries(index, _):
        dx, step = index // (NZ * NY), index % (NZ * NY)
        dz = step % NZ
        other, device = partner(dz, (dz + step // NZ) % NY, dx)
        remote(
            head(q_ref, other), q_buf.at[0, dx, z, y], q_send.at[dx], q_recv.at[dx], device
        ).start()
        return 0

    for chunk in range(CHUNKS):
        for slot, (dz, _, dx) in enumerate(STEPS[chunk]):
            group_ref[chunk * SLOTS + slot] = ((pipe + dx) % 2) * GPS + (z + NZ - dz) % NZ
    for section in range(2):
        for group in range(GPS):
            when = section
            for turn in range(GPS):
                when = when + jnp.where(order_ref[section, turn] == group, turn, 0)
            time_ref[section * GPS + group] = when

    send_kv(0)
    own_kv = []
    for number, (ref, kind, version) in enumerate(kv_refs()):
        copy = pltpu.make_async_copy(
            head(ref, seq), kv_buf.at[0, tp, 0, kind, version], local_sem.at[1 + number]
        )
        copy.start()
        own_kv.append(copy)
    own_q = pltpu.make_async_copy(head(q_ref, seq), q_buf.at[0, 0, z, y], local_sem.at[0])
    own_q.start()
    lax.fori_loop(1, NZ * NY, send_queries, 0)

    def clear(index, _):
        acc[index] = jnp.zeros(acc.shape[1:], jnp.float32)
        peak[index] = jnp.full(peak.shape[1:], START, jnp.float32)
        return 0

    lax.fori_loop(0, 4 * NZ, clear, 0)

    def forward_q(dx):
        return remote(q_buf.at[0, dx], q_buf.at[1, dx], qf_send.at[dx], qf_recv.at[dx], across)

    def forward_kv(chunk):
        mine = kv_buf.at[chunk, tp]
        return remote(mine, mine, fwd_send.at[chunk], fwd_recv.at[chunk], sibling)

    def blocks(count):
        return out_ref.at[:, pl.ds(0, count * HD)]

    bytes_of(kv_buf.at[0, tp, pl.ds(1, SLOTS - 1)], kv_recv.at[0])
    for copy in own_kv:
        copy.wait()
    forward_kv(0).start()
    lax.fori_loop(NZ * NY, CHUNKS * SLOTS, send_queries, 0)
    own_q.wait()
    bytes_of(blocks(NZ * NY - 1), q_recv.at[0])
    forward_q(0).start()
    send_kv(1)
    forward_kv(0).wait_recv()

    ones = jnp.ones((chunk_keys, HD), jnp.bfloat16)

    def chosen(chunk, kind, query_group):
        pieces = []
        for slot in range(SLOTS):
            key_group = group_ref[chunk * SLOTS + slot]
            fresh = jnp.logical_or(
                time_ref[key_group] < time_ref[query_group], key_group == query_group
            )
            for core in range(2):
                pieces.append(
                    jnp.where(
                        fresh,
                        kv_buf[chunk, core, slot, kind, 0],
                        kv_buf[chunk, core, slot, kind, 1],
                    )
                )
        return jnp.concatenate(pieces, axis=0)

    def attend(chunk, half, dx):
        first = (half * NX + dx) * NZ
        query_pipe = (pipe + dx + half) % 2

        def score(number):
            queries = q_buf[half, dx, number].reshape(block, HD)
            keys = chosen(chunk, 0, query_pipe * GPS + number)
            return lax.dot_general(
                queries, keys, (((1,), (1,)), ((), ())), preferred_element_type=jnp.float32
            )

        scores = score(0)
        for number in range(NZ):
            later = score(number + 1) if number + 1 < NZ else None
            values = chosen(chunk, 1, query_pipe * GPS + number)
            values = jnp.concatenate([values, ones], axis=1)
            before = peak[first + number, :, :1]
            now = jnp.maximum(before, jnp.max(scores, axis=1, keepdims=True) * scaling)
            weights = jnp.exp2(scores * scaling - now).astype(jnp.bfloat16)
            factor = jnp.exp2(before - now)
            acc[first + number] = acc[first + number] * factor + jnp.dot(
                weights, values, preferred_element_type=jnp.float32
            )
            peak[first + number] = jnp.broadcast_to(now, (block, HD))
            scores = later

    def finished(index):
        total = acc[index, :, HD : HD + 1]
        level = peak[index, :, :1] + jnp.log2(total)
        return acc[index, :, :HD] / total, level

    def exchange(dx):
        return (
            remote(part_out.at[dx], part_in.at[dx], part_send.at[dx], part_recv.at[dx], across),
            remote(lse_out.at[dx], lse_in.at[dx], lse_send.at[dx], lse_recv.at[dx], across),
        )

    def hand_over(dx):
        for number in range(NZ):
            mixed, level = finished((NX + dx) * NZ + number)
            part_out[dx, number] = mixed.astype(jnp.bfloat16)
            wide = jnp.concatenate(
                [
                    jnp.broadcast_to(level, (block, HD)),
                    jnp.zeros((lse_out.shape[3] - block, HD), jnp.float32),
                ],
                axis=0,
            )
            lse_out[dx, number] = jnp.transpose(wide)[:8]
        for copy in exchange(dx):
            copy.start()

    def give_back(dx):
        for copy in exchange(dx):
            copy.wait_recv()
        for number in range(NZ):
            mine, level = finished(dx * NZ + number)
            wide = jnp.concatenate([lse_in[dx, number]] * (HD // 8), axis=0)
            other_level = jnp.transpose(wide)[:block, :1]
            top = jnp.maximum(level, other_level)
            share, other_share = jnp.exp2(level - top), jnp.exp2(other_level - top)
            both = 1.0 / (share + other_share)
            mixed = mine * (share * both) + part_in[dx, number].astype(jnp.float32) * (
                other_share * both
            )
            done_buf[dx, number] = mixed.astype(jnp.bfloat16).reshape(NY, rows, HD)

            def send_back(back_y, _):
                other = (number * NY + back_y) * NX + (x + dx) % NX
                target = {"seq": other, "pipe": (pipe + dx) % 2}

                @pl.when(jnp.logical_or(other != seq, dx != 0))
                def _():
                    remote(
                        done_buf.at[dx, number, back_y], head(out_ref, seq),
                        done_send, done_recv, target,
                    ).start()

                return 0

            lax.fori_loop(0, NY, send_back, 0)

    def step(index, _):
        half, dx, chunk = (lookup(index, [entry[at] for entry in ORDER]) for at in range(3))

        @pl.when(index == 1)
        def _():
            bytes_of(blocks(NZ * NY), q_recv.at[1])
            forward_q(1).start()

        @pl.when(jnp.logical_or(index == 2, index == 5))
        def _():
            forward_q(dx).wait_recv()

        for at, number in ((3, 1), (6, 2), (8, 3)):

            @pl.when(index == at)
            def _():
                bytes_of(kv_buf.at[number, tp], kv_recv.at[number])
                forward_kv(number).start()

        for at, number in ((3, 1), (8, 2), (10, 3)):

            @pl.when(index == at)
            def _():
                forward_kv(number).wait_recv()

        @pl.when(index == 2)
        def _():
            send_kv(2)

        @pl.when(index == 4)
        def _():
            send_kv(3)

        attend(chunk, half, dx)

        @pl.when(jnp.logical_or(index == 10, index == 11))
        def _():
            hand_over(dx)

        @pl.when(jnp.logical_or(index == 13, index == 15))
        def _():
            give_back(dx)

        return 0

    lax.fori_loop(0, 4 * CHUNKS, step, 0)

    own_out = pltpu.make_async_copy(done_buf.at[0, z, y], head(out_ref, seq), local_sem.at[5])
    own_out.start()
    own_out.wait()
    for dx in range(NX):
        bytes_of(blocks(NZ * NY - 1 + dx), q_send.at[dx])
        forward_q(dx).wait_send()
    bytes_of(kv_buf.at[0, tp, pl.ds(1, SLOTS - 1)], kv_send.at[0])
    for chunk in range(1, CHUNKS):
        bytes_of(kv_buf.at[chunk, tp], kv_send.at[chunk])
    for chunk in range(CHUNKS):
        forward_kv(chunk).wait_send()
    for dx in range(NX):
        for copy in exchange(dx):
            copy.wait_send()
    bytes_of(blocks(CHUNKS * SLOTS - 1), done_send)
    bytes_of(blocks(CHUNKS * SLOTS - 1), done_recv)


def local(queries, keys, values, stale_keys, stale_values, group_order):
    rows, columns = queries.shape
    block = NY * rows
    dma = pltpu.SemaphoreType.DMA
    anywhere = pl.BlockSpec(memory_space=pl.ANY)
    return pl.pallas_call(
        kernel,
        out_shape=jax.ShapeDtypeStruct((rows, columns), jnp.bfloat16),
        in_specs=[pl.BlockSpec(memory_space=pltpu.SMEM)] + [anywhere] * 5,
        out_specs=anywhere,
        scratch_shapes=[
            pltpu.VMEM((2, NX, NZ, NY, rows, HD), jnp.bfloat16),
            pltpu.VMEM((CHUNKS, 2, SLOTS, 2, 2, rows, HD), jnp.bfloat16),
            pltpu.VMEM((2 * NX * NZ, block, 2 * HD), jnp.float32),
            pltpu.VMEM((2 * NX * NZ, block, HD), jnp.float32),
            pltpu.VMEM((NX, NZ, block, HD), jnp.bfloat16),
            pltpu.VMEM((NX, NZ, block, HD), jnp.bfloat16),
            pltpu.VMEM((NX, NZ, 8, 512), jnp.float32),
            pltpu.VMEM((NX, NZ, 8, 512), jnp.float32),
            pltpu.VMEM((NX, NZ, NY, rows, HD), jnp.bfloat16),
            pltpu.SMEM((2 * GPS,), jnp.int32),
            pltpu.SMEM((CHUNKS * SLOTS,), jnp.int32),
            dma((6,)), dma((NX,)), dma((NX,)), dma((NX,)), dma((NX,)),
            dma((CHUNKS,)), dma((CHUNKS,)), dma((CHUNKS,)), dma((CHUNKS,)),
            dma((NX,)), dma((NX,)), dma((NX,)), dma((NX,)), dma, dma,
        ],
        compiler_params=pltpu.CompilerParams(
            collective_id=0, has_side_effects=True, vmem_limit_bytes=60 * 2**20
        ),
    )(group_order, queries, keys, values, stale_keys, stale_values)


def solution(mesh):
    placed = P(("pipe", "seq", "tp"), None)
    return jax.shard_map(
        local, mesh=mesh, in_specs=(placed,) * 5 + (P(),), out_specs=placed, check_vma=False
    )
```

```python
import functools
import math

import jax
import jax.numpy as jnp
from jax import lax
from jax.experimental import pallas as pl
from jax.experimental.pallas import tpu as pltpu
from jax.sharding import PartitionSpec as P

MESH = pl.DeviceIdType.MESH
GPS = 4
HD = 128
NZ, NY, NX = 4, 4, 2
SLOTS = NZ * NX
CHUNKS = NY
START = -1e30


STEPS = (
    ((0, 0, 0), (0, 0, 1), (1, 0, 0), (3, 0, 0), (0, 1, 0), (0, 3, 0), (1, 1, 1), (3, 3, 0)),
    ((0, 2, 0), (3, 1, 1), (2, 0, 1), (3, 1, 0), (2, 3, 0), (1, 3, 1), (0, 1, 1), (1, 3, 0)),
    ((2, 0, 0), (0, 3, 1), (3, 2, 0), (0, 2, 1), (2, 1, 1), (1, 0, 1), (2, 2, 0), (2, 2, 1)),
    ((3, 3, 1), (2, 1, 0), (1, 1, 0), (2, 3, 1), (1, 2, 0), (3, 2, 1), (3, 0, 1), (1, 2, 1)),
)
ORDER = (
    (0, 0, 0), (0, 1, 0), (1, 0, 0), (1, 1, 0), (0, 0, 1), (0, 1, 1), (1, 0, 1), (1, 1, 1),
    (1, 0, 2), (1, 1, 2), (1, 0, 3), (1, 1, 3), (0, 0, 2), (0, 0, 3), (0, 1, 2), (0, 1, 3),
)


def lookup(index, table):
    found = table[0]
    for at in range(1, len(table)):
        if table[at] != table[at - 1]:
            found = jnp.where(index >= at, table[at], found)
    return found


def kernel(
    order_ref, q_ref, k_ref, v_ref, sk_ref, sv_ref, out_ref,
    q_buf, kv_buf, acc, peak, part_out, part_in, lse_out, lse_in, done_buf,
    time_ref, group_ref,
    local_sem, q_send, q_recv, qf_send, qf_recv, kv_send, kv_recv, fwd_send, fwd_recv,
    part_send, part_recv, lse_send, lse_recv, done_send, done_recv,
):
    pipe, seq, tp = lax.axis_index("pipe"), lax.axis_index("seq"), lax.axis_index("tp")
    z, y, x = seq // (NY * NX), (seq // NX) % NY, seq % NX
    rows = q_ref.shape[0]
    block = NY * rows
    chunk_keys = 2 * SLOTS * rows
    scaling = math.log2(math.e) / math.sqrt(HD)
    sibling = {"tp": 1 - tp}
    across = {"pipe": 1 - pipe}

    def partner(dz, dy, dx):
        other = (((z + dz) % NZ) * NY + (y + dy) % NY) * NX + (x + dx) % NX
        return other, {"seq": other, "pipe": (pipe + dx) % 2}

    def remote(src, dst, send, recv, device):
        return pltpu.make_async_remote_copy(
            src_ref=src, dst_ref=dst, send_sem=send, recv_sem=recv,
            device_id=device, device_id_type=MESH,
        )

    def bytes_of(view, sem):
        pltpu.make_async_copy(view, view, sem).wait()

    barrier = pltpu.get_barrier_semaphore()

    def greet(index, _):
        _, device = partner(index // (NY * NX), (index // NX) % NY, index % NX)
        pl.semaphore_signal(barrier, inc=1, device_id=device, device_id_type=MESH)
        return 0

    lax.fori_loop(1, CHUNKS * SLOTS, greet, 0)
    pl.semaphore_signal(barrier, inc=1, device_id=sibling, device_id_type=MESH)
    pl.semaphore_signal(barrier, inc=1, device_id=across, device_id_type=MESH)
    pl.semaphore_wait(barrier, CHUNKS * SLOTS + 1)

    def head(ref, which):
        return ref.at[:, pl.ds(pl.multiple_of(which * HD, HD), HD)]

    def kv_refs():
        return ((k_ref, 0, 0), (sk_ref, 0, 1), (v_ref, 1, 0), (sv_ref, 1, 1))

    def send_kv(chunk):
        for slot, step in enumerate(STEPS[chunk]):
            if step == (0, 0, 0):
                continue
            other, device = partner(*step)
            for ref, kind, version in kv_refs():
                remote(
                    head(ref, other), kv_buf.at[chunk, tp, slot, kind, version],
                    kv_send.at[chunk], kv_recv.at[chunk], device,
                ).start()

    def send_queries(index, _):
        dx, step = index // (NZ * NY), index % (NZ * NY)
        dz = step % NZ
        other, device = partner(dz, (dz + step // NZ) % NY, dx)
        remote(
            head(q_ref, other), q_buf.at[0, dx, z, y], q_send.at[dx], q_recv.at[dx], device
        ).start()
        return 0

    for chunk in range(CHUNKS):
        for slot, (dz, _, dx) in enumerate(STEPS[chunk]):
            group_ref[chunk * SLOTS + slot] = ((pipe + dx) % 2) * GPS + (z + NZ - dz) % NZ
    for section in range(2):
        for group in range(GPS):
            when = section
            for turn in range(GPS):
                when = when + jnp.where(order_ref[section, turn] == group, turn, 0)
            time_ref[section * GPS + group] = when

    send_kv(0)
    own_kv = []
    for number, (ref, kind, version) in enumerate(kv_refs()):
        copy = pltpu.make_async_copy(
            head(ref, seq), kv_buf.at[0, tp, 0, kind, version], local_sem.at[1 + number]
        )
        copy.start()
        own_kv.append(copy)
    own_q = pltpu.make_async_copy(head(q_ref, seq), q_buf.at[0, 0, z, y], local_sem.at[0])
    own_q.start()
    lax.fori_loop(1, CHUNKS * SLOTS, send_queries, 0)

    def clear(index, _):
        acc[index] = jnp.zeros(acc.shape[1:], jnp.float32)
        peak[index] = jnp.full(peak.shape[1:], START, jnp.float32)
        return 0

    lax.fori_loop(0, 4 * NZ, clear, 0)

    def forward_q(dx):
        return remote(q_buf.at[0, dx], q_buf.at[1, dx], qf_send.at[dx], qf_recv.at[dx], across)

    def forward_kv(chunk):
        mine = kv_buf.at[chunk, tp]
        return remote(mine, mine, fwd_send.at[chunk], fwd_recv.at[chunk], sibling)

    def blocks(count):
        return out_ref.at[:, pl.ds(0, count * HD)]

    bytes_of(kv_buf.at[0, tp, pl.ds(1, SLOTS - 1)], kv_recv.at[0])
    for copy in own_kv:
        copy.wait()
    forward_kv(0).start()
    send_kv(1)
    own_q.wait()
    bytes_of(blocks(NZ * NY - 1), q_recv.at[0])
    forward_q(0).start()
    forward_kv(0).wait_recv()

    ones = jnp.ones((chunk_keys, HD), jnp.bfloat16)

    def chosen(chunk, kind, query_group):
        pieces = []
        for slot in range(SLOTS):
            key_group = group_ref[chunk * SLOTS + slot]
            fresh = jnp.logical_or(
                time_ref[key_group] < time_ref[query_group], key_group == query_group
            )
            for core in range(2):
                pieces.append(
                    jnp.where(
                        fresh,
                        kv_buf[chunk, core, slot, kind, 0],
                        kv_buf[chunk, core, slot, kind, 1],
                    )
                )
        return jnp.concatenate(pieces, axis=0)

    def attend(chunk, half, dx):
        first = (half * NX + dx) * NZ
        query_pipe = (pipe + dx + half) % 2

        def score(number):
            queries = q_buf[half, dx, number].reshape(block, HD)
            keys = chosen(chunk, 0, query_pipe * GPS + number)
            return lax.dot_general(
                queries, keys, (((1,), (1,)), ((), ())), preferred_element_type=jnp.float32
            )

        scores = score(0)
        for number in range(NZ):
            later = score(number + 1) if number + 1 < NZ else None
            values = chosen(chunk, 1, query_pipe * GPS + number)
            values = jnp.concatenate([values, ones], axis=1)
            before = peak[first + number, :, :1]
            now = jnp.maximum(before, jnp.max(scores, axis=1, keepdims=True) * scaling)
            weights = jnp.exp2(scores * scaling - now).astype(jnp.bfloat16)
            factor = jnp.exp2(before - now)
            acc[first + number] = acc[first + number] * factor + jnp.dot(
                weights, values, preferred_element_type=jnp.float32
            )
            peak[first + number] = jnp.broadcast_to(now, (block, HD))
            scores = later

    def finished(index):
        total = acc[index, :, HD : HD + 1]
        level = peak[index, :, :1] + jnp.log2(total)
        return acc[index, :, :HD] / total, level

    def exchange(dx):
        return (
            remote(part_out.at[dx], part_in.at[dx], part_send.at[dx], part_recv.at[dx], across),
            remote(lse_out.at[dx], lse_in.at[dx], lse_send.at[dx], lse_recv.at[dx], across),
        )

    def hand_over(dx):
        for number in range(NZ):
            mixed, level = finished((NX + dx) * NZ + number)
            part_out[dx, number] = mixed.astype(jnp.bfloat16)
            wide = jnp.concatenate(
                [
                    jnp.broadcast_to(level, (block, HD)),
                    jnp.zeros((lse_out.shape[3] - block, HD), jnp.float32),
                ],
                axis=0,
            )
            lse_out[dx, number] = jnp.transpose(wide)[:8]
        for copy in exchange(dx):
            copy.start()

    def give_back(dx):
        for copy in exchange(dx):
            copy.wait_recv()
        for number in range(NZ):
            mine, level = finished(dx * NZ + number)
            wide = jnp.concatenate([lse_in[dx, number]] * (HD // 8), axis=0)
            other_level = jnp.transpose(wide)[:block, :1]
            top = jnp.maximum(level, other_level)
            share, other_share = jnp.exp2(level - top), jnp.exp2(other_level - top)
            both = 1.0 / (share + other_share)
            mixed = mine * (share * both) + part_in[dx, number].astype(jnp.float32) * (
                other_share * both
            )
            done_buf[dx, number] = mixed.astype(jnp.bfloat16).reshape(NY, rows, HD)

            def send_back(back_y, _):
                other = (number * NY + back_y) * NX + (x + dx) % NX
                target = {"seq": other, "pipe": (pipe + dx) % 2}

                @pl.when(jnp.logical_or(other != seq, dx != 0))
                def _():
                    remote(
                        done_buf.at[dx, number, back_y], head(out_ref, seq),
                        done_send, done_recv, target,
                    ).start()

                return 0

            lax.fori_loop(0, NY, send_back, 0)

    def step(index, _):
        half, dx, chunk = (lookup(index, [entry[at] for entry in ORDER]) for at in range(3))

        for at, number in ((1, 2), (3, 3)):

            @pl.when(index == at)
            def _():
                send_kv(number)

        @pl.when(index == 1)
        def _():
            bytes_of(blocks(NZ * NY), q_recv.at[1])
            forward_q(1).start()

        @pl.when(jnp.logical_or(index == 2, index == 3))
        def _():
            forward_q(dx).wait_recv()

        for at, number in ((3, 1), (7, 2), (9, 3)):

            @pl.when(index == at)
            def _():
                bytes_of(kv_buf.at[number, tp], kv_recv.at[number])
                forward_kv(number).start()

        for at, number in ((4, 1), (8, 2), (10, 3)):

            @pl.when(index == at)
            def _():
                forward_kv(number).wait_recv()

        attend(chunk, half, dx)

        @pl.when(jnp.logical_or(index == 10, index == 11))
        def _():
            hand_over(dx)

        @pl.when(jnp.logical_or(index == 13, index == 15))
        def _():
            give_back(dx)

        return 0

    lax.fori_loop(0, 4 * CHUNKS, step, 0)

    own_out = pltpu.make_async_copy(done_buf.at[0, z, y], head(out_ref, seq), local_sem.at[5])
    own_out.start()
    own_out.wait()
    for dx in range(NX):
        bytes_of(blocks(NZ * NY - 1 + dx), q_send.at[dx])
        forward_q(dx).wait_send()
    bytes_of(kv_buf.at[0, tp, pl.ds(1, SLOTS - 1)], kv_send.at[0])
    for chunk in range(1, CHUNKS):
        bytes_of(kv_buf.at[chunk, tp], kv_send.at[chunk])
    for chunk in range(CHUNKS):
        forward_kv(chunk).wait_send()
    for dx in range(NX):
        for copy in exchange(dx):
            copy.wait_send()
    bytes_of(blocks(CHUNKS * SLOTS - 1), done_send)
    bytes_of(blocks(CHUNKS * SLOTS - 1), done_recv)


def local(queries, keys, values, stale_keys, stale_values, group_order):
    rows, columns = queries.shape
    block = NY * rows
    dma = pltpu.SemaphoreType.DMA
    anywhere = pl.BlockSpec(memory_space=pl.ANY)
    return pl.pallas_call(
        kernel,
        out_shape=jax.ShapeDtypeStruct((rows, columns), jnp.bfloat16),
        in_specs=[pl.BlockSpec(memory_space=pltpu.SMEM)] + [anywhere] * 5,
        out_specs=anywhere,
        scratch_shapes=[
            pltpu.VMEM((2, NX, NZ, NY, rows, HD), jnp.bfloat16),
            pltpu.VMEM((CHUNKS, 2, SLOTS, 2, 2, rows, HD), jnp.bfloat16),
            pltpu.VMEM((2 * NX * NZ, block, 2 * HD), jnp.float32),
            pltpu.VMEM((2 * NX * NZ, block, HD), jnp.float32),
            pltpu.VMEM((NX, NZ, block, HD), jnp.bfloat16),
            pltpu.VMEM((NX, NZ, block, HD), jnp.bfloat16),
            pltpu.VMEM((NX, NZ, 8, 512), jnp.float32),
            pltpu.VMEM((NX, NZ, 8, 512), jnp.float32),
            pltpu.VMEM((NX, NZ, NY, rows, HD), jnp.bfloat16),
            pltpu.SMEM((2 * GPS,), jnp.int32),
            pltpu.SMEM((CHUNKS * SLOTS,), jnp.int32),
            dma((6,)), dma((NX,)), dma((NX,)), dma((NX,)), dma((NX,)),
            dma((CHUNKS,)), dma((CHUNKS,)), dma((CHUNKS,)), dma((CHUNKS,)),
            dma((NX,)), dma((NX,)), dma((NX,)), dma((NX,)), dma, dma,
        ],
        compiler_params=pltpu.CompilerParams(
            collective_id=0, has_side_effects=True, vmem_limit_bytes=60 * 2**20
        ),
    )(group_order, queries, keys, values, stale_keys, stale_values)


def solution(mesh):
    placed = P(("pipe", "seq", "tp"), None)
    return jax.shard_map(
        local, mesh=mesh, in_specs=(placed,) * 5 + (P(),), out_specs=placed, check_vma=False
    )
```

```python
import functools
import math

import jax
import jax.numpy as jnp
from jax import lax
from jax.experimental import pallas as pl
from jax.experimental.pallas import tpu as pltpu
from jax.sharding import PartitionSpec as P

MESH = pl.DeviceIdType.MESH
GPS = 4
HD = 128
NZ, NY, NX = 4, 4, 2
SLOTS = NZ * NX
CHUNKS = NY
START = -1e30


STEPS = (
    ((0, 0, 0), (0, 0, 1), (1, 0, 0), (3, 0, 0), (0, 1, 0), (0, 3, 0), (1, 1, 1), (3, 3, 0)),
    ((0, 2, 0), (3, 1, 1), (2, 0, 1), (3, 1, 0), (2, 3, 0), (1, 3, 1), (0, 1, 1), (1, 3, 0)),
    ((2, 0, 0), (0, 3, 1), (3, 2, 0), (0, 2, 1), (2, 1, 1), (1, 0, 1), (2, 2, 0), (2, 2, 1)),
    ((3, 3, 1), (2, 1, 0), (1, 1, 0), (2, 3, 1), (1, 2, 0), (3, 2, 1), (3, 0, 1), (1, 2, 1)),
)
ORDER = (
    (0, 0, 0), (0, 1, 0), (1, 0, 0), (1, 1, 0), (0, 0, 1), (0, 1, 1), (1, 0, 1), (1, 1, 1),
    (1, 0, 2), (1, 1, 2), (1, 0, 3), (1, 1, 3), (0, 0, 2), (0, 0, 3), (0, 1, 2), (0, 1, 3),
)


def lookup(index, table):
    found = table[0]
    for at in range(1, len(table)):
        if table[at] != table[at - 1]:
            found = jnp.where(index >= at, table[at], found)
    return found


def kernel(
    order_ref, q_ref, k_ref, v_ref, sk_ref, sv_ref, out_ref,
    q_buf, kv_buf, acc, peak, part_out, part_in, lse_out, lse_in, done_buf,
    time_ref, group_ref,
    local_sem, q_send, q_recv, qf_send, qf_recv, kv_send, kv_recv, fwd_send, fwd_recv,
    part_send, part_recv, lse_send, lse_recv, done_send, done_recv,
):
    pipe, seq, tp = lax.axis_index("pipe"), lax.axis_index("seq"), lax.axis_index("tp")
    z, y, x = seq // (NY * NX), (seq // NX) % NY, seq % NX
    rows = q_ref.shape[0]
    block = NY * rows
    chunk_keys = 2 * SLOTS * rows
    scaling = math.log2(math.e) / math.sqrt(HD)
    sibling = {"tp": 1 - tp}
    across = {"pipe": 1 - pipe}

    def partner(dz, dy, dx):
        other = (((z + dz) % NZ) * NY + (y + dy) % NY) * NX + (x + dx) % NX
        return other, {"seq": other, "pipe": (pipe + dx) % 2}

    def remote(src, dst, send, recv, device):
        return pltpu.make_async_remote_copy(
            src_ref=src, dst_ref=dst, send_sem=send, recv_sem=recv,
            device_id=device, device_id_type=MESH,
        )

    def bytes_of(view, sem):
        pltpu.make_async_copy(view, view, sem).wait()

    barrier = pltpu.get_barrier_semaphore()

    def greet(index, _):
        _, device = partner(index // (NY * NX), (index // NX) % NY, index % NX)
        pl.semaphore_signal(barrier, inc=1, device_id=device, device_id_type=MESH)
        return 0

    lax.fori_loop(1, CHUNKS * SLOTS, greet, 0)
    pl.semaphore_signal(barrier, inc=1, device_id=sibling, device_id_type=MESH)
    pl.semaphore_signal(barrier, inc=1, device_id=across, device_id_type=MESH)
    for chunk in range(CHUNKS):
        for slot, (dz, _, dx) in enumerate(STEPS[chunk]):
            group_ref[chunk * SLOTS + slot] = ((pipe + dx) % 2) * GPS + (z + NZ - dz) % NZ
    for section in range(2):
        for group in range(GPS):
            when = section
            for turn in range(GPS):
                when = when + jnp.where(order_ref[section, turn] == group, turn, 0)
            time_ref[section * GPS + group] = when

    pl.semaphore_wait(barrier, CHUNKS * SLOTS + 1)

    def head(ref, which):
        return ref.at[:, pl.ds(pl.multiple_of(which * HD, HD), HD)]

    def kv_refs():
        return ((k_ref, 0, 0), (sk_ref, 0, 1), (v_ref, 1, 0), (sv_ref, 1, 1))

    def send_kv(chunk):
        for slot, step in enumerate(STEPS[chunk]):
            if step == (0, 0, 0):
                continue
            other, device = partner(*step)
            for ref, kind, version in kv_refs():
                remote(
                    head(ref, other), kv_buf.at[chunk, tp, slot, kind, version],
                    kv_send.at[chunk], kv_recv.at[chunk], device,
                ).start()

    def send_queries(index, _):
        dx, step = index // (NZ * NY), index % (NZ * NY)
        dz = step % NZ
        other, device = partner(dz, (dz + step // NZ) % NY, dx)
        remote(
            head(q_ref, other), q_buf.at[0, dx, z, y], q_send.at[dx], q_recv.at[dx], device
        ).start()
        return 0

    lax.fori_loop(1, CHUNKS * SLOTS, send_queries, 0)
    send_kv(0)
    own_q = pltpu.make_async_copy(head(q_ref, seq), q_buf.at[0, 0, z, y], local_sem.at[0])
    own_q.start()
    own_kv = []
    for number, (ref, kind, version) in enumerate(kv_refs()):
        copy = pltpu.make_async_copy(
            head(ref, seq), kv_buf.at[0, tp, 0, kind, version], local_sem.at[1 + number]
        )
        copy.start()
        own_kv.append(copy)

    def clear(index, _):
        acc[index] = jnp.zeros(acc.shape[1:], jnp.float32)
        peak[index] = jnp.full(peak.shape[1:], START, jnp.float32)
        return 0

    lax.fori_loop(0, 4 * NZ, clear, 0)

    def forward_q(dx):
        return remote(q_buf.at[0, dx], q_buf.at[1, dx], qf_send.at[dx], qf_recv.at[dx], across)

    def forward_kv(chunk):
        mine = kv_buf.at[chunk, tp]
        return remote(mine, mine, fwd_send.at[chunk], fwd_recv.at[chunk], sibling)

    def blocks(count):
        return out_ref.at[:, pl.ds(0, count * HD)]

    own_q.wait()
    for dx in range(NX):
        bytes_of(blocks(NZ * NY - 1 + dx), q_recv.at[dx])
        forward_q(dx).start()
    bytes_of(kv_buf.at[0, tp, pl.ds(1, SLOTS - 1)], kv_recv.at[0])
    for copy in own_kv:
        copy.wait()
    forward_kv(0).start()
    send_kv(1)
    send_kv(2)
    forward_kv(0).wait_recv()

    ones = jnp.ones((chunk_keys, HD), jnp.bfloat16)

    def chosen(chunk, kind, query_group):
        pieces = []
        for slot in range(SLOTS):
            key_group = group_ref[chunk * SLOTS + slot]
            fresh = jnp.logical_or(
                time_ref[key_group] < time_ref[query_group], key_group == query_group
            )
            for core in range(2):
                pieces.append(
                    jnp.where(
                        fresh,
                        kv_buf[chunk, core, slot, kind, 0],
                        kv_buf[chunk, core, slot, kind, 1],
                    )
                )
        return jnp.concatenate(pieces, axis=0)

    def attend(chunk, half, dx):
        first = (half * NX + dx) * NZ
        query_pipe = (pipe + dx + half) % 2

        def score(number):
            queries = q_buf[half, dx, number].reshape(block, HD)
            keys = chosen(chunk, 0, query_pipe * GPS + number)
            return lax.dot_general(
                queries, keys, (((1,), (1,)), ((), ())), preferred_element_type=jnp.float32
            )

        scores = score(0)
        for number in range(NZ):
            later = score(number + 1) if number + 1 < NZ else None
            values = chosen(chunk, 1, query_pipe * GPS + number)
            values = jnp.concatenate([values, ones], axis=1)
            before = peak[first + number, :, :1]
            now = jnp.maximum(before, jnp.max(scores, axis=1, keepdims=True) * scaling)
            weights = jnp.exp2(scores * scaling - now).astype(jnp.bfloat16)
            factor = jnp.exp2(before - now)
            acc[first + number] = acc[first + number] * factor + jnp.dot(
                weights, values, preferred_element_type=jnp.float32
            )
            peak[first + number] = jnp.broadcast_to(now, (block, HD))
            scores = later

    def finished(index):
        total = acc[index, :, HD : HD + 1]
        level = peak[index, :, :1] + jnp.log2(total)
        return acc[index, :, :HD] / total, level

    def exchange(dx):
        return (
            remote(part_out.at[dx], part_in.at[dx], part_send.at[dx], part_recv.at[dx], across),
            remote(lse_out.at[dx], lse_in.at[dx], lse_send.at[dx], lse_recv.at[dx], across),
        )

    def hand_over(dx):
        lane = lax.broadcasted_iota(jnp.int32, (block, HD), 1)
        levels = jnp.zeros((block, HD), jnp.float32)
        for number in range(NZ):
            mixed, level = finished((NX + dx) * NZ + number)
            part_out[dx, number] = mixed.astype(jnp.bfloat16)
            remote(
                part_out.at[dx, number], part_in.at[dx, number],
                part_send.at[dx], part_recv.at[dx], across,
            ).start()
            levels = jnp.where(lane == number, level, levels)
        wide = jnp.concatenate(
            [levels, jnp.zeros((lse_out.shape[2] - block, HD), jnp.float32)], axis=0
        )
        lse_out[dx] = jnp.transpose(wide)[:8]
        remote(
            lse_out.at[dx], lse_in.at[dx], lse_send.at[dx], lse_recv.at[dx], across
        ).start()

    def give_back(dx):
        for copy in exchange(dx):
            copy.wait_recv()
        other_levels = jnp.transpose(jnp.concatenate([lse_in[dx]] * (HD // 8), axis=0))[:block]
        for number in range(NZ):
            mine, level = finished(dx * NZ + number)
            other_level = other_levels[:, number : number + 1]
            top = jnp.maximum(level, other_level)
            share, other_share = jnp.exp2(level - top), jnp.exp2(other_level - top)
            both = 1.0 / (share + other_share)
            mixed = mine * (share * both) + part_in[dx, number].astype(jnp.float32) * (
                other_share * both
            )
            done_buf[dx, number] = mixed.astype(jnp.bfloat16).reshape(NY, rows, HD)

            def send_back(back_y, _):
                other = (number * NY + back_y) * NX + (x + dx) % NX
                target = {"seq": other, "pipe": (pipe + dx) % 2}

                @pl.when(jnp.logical_or(other != seq, dx != 0))
                def _():
                    remote(
                        done_buf.at[dx, number, back_y], head(out_ref, seq),
                        done_send, done_recv, target,
                    ).start()

                return 0

            lax.fori_loop(0, NY, send_back, 0)

    def step(index, _):
        half, dx, chunk = (lookup(index, [entry[at] for entry in ORDER]) for at in range(3))

        for at, number in ((5, 3),):

            @pl.when(index == at)
            def _():
                send_kv(number)

        @pl.when(jnp.logical_or(index == 2, index == 3))
        def _():
            forward_q(dx).wait_recv()

        for at, number in ((3, 1), (7, 2), (9, 3)):

            @pl.when(index == at)
            def _():
                bytes_of(kv_buf.at[number, tp], kv_recv.at[number])
                forward_kv(number).start()

        for at, number in ((4, 1), (8, 2), (10, 3)):

            @pl.when(index == at)
            def _():
                forward_kv(number).wait_recv()

        attend(chunk, half, dx)

        @pl.when(jnp.logical_or(index == 10, index == 11))
        def _():
            hand_over(dx)

        @pl.when(jnp.logical_or(index == 13, index == 15))
        def _():
            give_back(dx)

        return 0

    lax.fori_loop(0, 4 * CHUNKS, step, 0)

    own_out = pltpu.make_async_copy(done_buf.at[0, z, y], head(out_ref, seq), local_sem.at[5])
    own_out.start()
    own_out.wait()
    for dx in range(NX):
        bytes_of(blocks(NZ * NY - 1 + dx), q_send.at[dx])
        forward_q(dx).wait_send()
    bytes_of(kv_buf.at[0, tp, pl.ds(1, SLOTS - 1)], kv_send.at[0])
    for chunk in range(1, CHUNKS):
        bytes_of(kv_buf.at[chunk, tp], kv_send.at[chunk])
    for chunk in range(CHUNKS):
        forward_kv(chunk).wait_send()
    for dx in range(NX):
        for copy in exchange(dx):
            copy.wait_send()
    bytes_of(blocks(CHUNKS * SLOTS - 1), done_send)
    bytes_of(blocks(CHUNKS * SLOTS - 1), done_recv)


def local(queries, keys, values, stale_keys, stale_values, group_order):
    rows, columns = queries.shape
    block = NY * rows
    dma = pltpu.SemaphoreType.DMA
    anywhere = pl.BlockSpec(memory_space=pl.ANY)
    return pl.pallas_call(
        kernel,
        out_shape=jax.ShapeDtypeStruct((rows, columns), jnp.bfloat16),
        in_specs=[pl.BlockSpec(memory_space=pltpu.SMEM)] + [anywhere] * 5,
        out_specs=anywhere,
        scratch_shapes=[
            pltpu.VMEM((2, NX, NZ, NY, rows, HD), jnp.bfloat16),
            pltpu.VMEM((CHUNKS, 2, SLOTS, 2, 2, rows, HD), jnp.bfloat16),
            pltpu.VMEM((2 * NX * NZ, block, 2 * HD), jnp.float32),
            pltpu.VMEM((2 * NX * NZ, block, HD), jnp.float32),
            pltpu.VMEM((NX, NZ, block, HD), jnp.bfloat16),
            pltpu.VMEM((NX, NZ, block, HD), jnp.bfloat16),
            pltpu.VMEM((NX, 8, 512), jnp.float32),
            pltpu.VMEM((NX, 8, 512), jnp.float32),
            pltpu.VMEM((NX, NZ, NY, rows, HD), jnp.bfloat16),
            pltpu.SMEM((2 * GPS,), jnp.int32),
            pltpu.SMEM((CHUNKS * SLOTS,), jnp.int32),
            dma((6,)), dma((NX,)), dma((NX,)), dma((NX,)), dma((NX,)),
            dma((CHUNKS,)), dma((CHUNKS,)), dma((CHUNKS,)), dma((CHUNKS,)),
            dma((NX,)), dma((NX,)), dma((NX,)), dma((NX,)), dma, dma,
        ],
        compiler_params=pltpu.CompilerParams(
            collective_id=0, has_side_effects=True, vmem_limit_bytes=60 * 2**20
        ),
    )(group_order, queries, keys, values, stale_keys, stale_values)


def solution(mesh):
    placed = P(("pipe", "seq", "tp"), None)
    return jax.shard_map(
        local, mesh=mesh, in_specs=(placed,) * 5 + (P(),), out_specs=placed, check_vma=False
    )
```

```python
import functools
import math

import jax
import jax.numpy as jnp
from jax import lax
from jax.experimental import pallas as pl
from jax.experimental.pallas import tpu as pltpu
from jax.sharding import PartitionSpec as P

MESH = pl.DeviceIdType.MESH
GPS = 4
HD = 128
NZ, NY, NX = 4, 4, 2
SLOTS = NZ * NX
CHUNKS = NY
START = -1e30


STEPS = (
    ((0, 0, 0), (0, 0, 1), (1, 0, 0), (3, 0, 0), (0, 1, 0), (0, 3, 0), (1, 1, 1), (3, 3, 0)),
    ((0, 2, 0), (3, 1, 1), (2, 0, 1), (3, 1, 0), (2, 3, 0), (1, 3, 1), (0, 1, 1), (1, 3, 0)),
    ((2, 0, 0), (0, 3, 1), (3, 2, 0), (0, 2, 1), (2, 1, 1), (1, 0, 1), (2, 2, 0), (2, 2, 1)),
    ((3, 3, 1), (2, 1, 0), (1, 1, 0), (2, 3, 1), (1, 2, 0), (3, 2, 1), (3, 0, 1), (1, 2, 1)),
)
ORDER = (
    (0, 0, 0), (0, 1, 0), (1, 0, 0), (1, 1, 0), (0, 0, 1), (0, 1, 1), (1, 0, 1), (1, 1, 1),
    (1, 0, 2), (1, 1, 2), (1, 0, 3), (1, 1, 3), (0, 0, 2), (0, 0, 3), (0, 1, 2), (0, 1, 3),
)


def lookup(index, table):
    found = table[0]
    for at in range(1, len(table)):
        if table[at] != table[at - 1]:
            found = jnp.where(index >= at, table[at], found)
    return found


def kernel(
    order_ref, q_ref, k_ref, v_ref, sk_ref, sv_ref, out_ref,
    q_buf, kv_buf, acc, peak, part_out, part_in, lse_out, lse_in, done_buf,
    time_ref, group_ref,
    local_sem, q_send, q_recv, qf_send, qf_recv, kv_send, kv_recv, fwd_send, fwd_recv,
    part_send, part_recv, lse_send, lse_recv, done_send, done_recv,
):
    pipe, seq, tp = lax.axis_index("pipe"), lax.axis_index("seq"), lax.axis_index("tp")
    z, y, x = seq // (NY * NX), (seq // NX) % NY, seq % NX
    rows = q_ref.shape[0]
    block = NY * rows
    chunk_keys = 2 * SLOTS * rows
    scaling = math.log2(math.e) / math.sqrt(HD)
    sibling = {"tp": 1 - tp}
    across = {"pipe": 1 - pipe}

    def partner(dz, dy, dx):
        other = (((z + dz) % NZ) * NY + (y + dy) % NY) * NX + (x + dx) % NX
        return other, {"seq": other, "pipe": (pipe + dx) % 2}

    def remote(src, dst, send, recv, device):
        return pltpu.make_async_remote_copy(
            src_ref=src, dst_ref=dst, send_sem=send, recv_sem=recv,
            device_id=device, device_id_type=MESH,
        )

    def bytes_of(view, sem):
        pltpu.make_async_copy(view, view, sem).wait()

    barrier = pltpu.get_barrier_semaphore()

    def greet(index, _):
        _, device = partner(index // (NY * NX), (index // NX) % NY, index % NX)
        pl.semaphore_signal(barrier, inc=1, device_id=device, device_id_type=MESH)
        return 0

    lax.fori_loop(1, CHUNKS * SLOTS, greet, 0)
    pl.semaphore_signal(barrier, inc=1, device_id=sibling, device_id_type=MESH)
    pl.semaphore_signal(barrier, inc=1, device_id=across, device_id_type=MESH)
    for chunk in range(CHUNKS):
        for slot, (dz, _, dx) in enumerate(STEPS[chunk]):
            group_ref[chunk * SLOTS + slot] = ((pipe + dx) % 2) * GPS + (z + NZ - dz) % NZ
    for section in range(2):
        for group in range(GPS):
            when = section
            for turn in range(GPS):
                when = when + jnp.where(order_ref[section, turn] == group, turn, 0)
            time_ref[section * GPS + group] = when

    pl.semaphore_wait(barrier, CHUNKS * SLOTS + 1)

    def head(ref, which):
        return ref.at[:, pl.ds(pl.multiple_of(which * HD, HD), HD)]

    def kv_refs():
        return ((k_ref, 0, 0), (sk_ref, 0, 1), (v_ref, 1, 0), (sv_ref, 1, 1))

    def send_kv(chunk):
        for slot, step in enumerate(STEPS[chunk]):
            if step == (0, 0, 0):
                continue
            other, device = partner(*step)
            for ref, kind, version in kv_refs():
                remote(
                    head(ref, other), kv_buf.at[chunk, tp, slot, kind, version],
                    kv_send.at[chunk], kv_recv.at[chunk], device,
                ).start()

    def send_queries(index, _):
        dx, step = index // (NZ * NY), index % (NZ * NY)
        dz = step % NZ
        other, device = partner(dz, (dz + step // NZ) % NY, dx)
        remote(
            head(q_ref, other), q_buf.at[0, dx, z, y], q_send.at[dx], q_recv.at[dx], device
        ).start()
        return 0

    lax.fori_loop(1, CHUNKS * SLOTS, send_queries, 0)
    send_kv(0)
    own_q = pltpu.make_async_copy(head(q_ref, seq), q_buf.at[0, 0, z, y], local_sem.at[0])
    own_q.start()
    own_kv = []
    for number, (ref, kind, version) in enumerate(kv_refs()):
        copy = pltpu.make_async_copy(
            head(ref, seq), kv_buf.at[0, tp, 0, kind, version], local_sem.at[1 + number]
        )
        copy.start()
        own_kv.append(copy)

    def clear(index, _):
        acc[index] = jnp.zeros(acc.shape[1:], jnp.float32)
        peak[index] = jnp.full(peak.shape[1:], START, jnp.float32)
        return 0

    lax.fori_loop(0, 4 * NZ, clear, 0)

    def forward_q(dx):
        return remote(q_buf.at[0, dx], q_buf.at[1, dx], qf_send.at[dx], qf_recv.at[dx], across)

    def forward_kv(chunk):
        mine = kv_buf.at[chunk, tp]
        return remote(mine, mine, fwd_send.at[chunk], fwd_recv.at[chunk], sibling)

    def blocks(count):
        return out_ref.at[:, pl.ds(0, count * HD)]

    own_q.wait()
    for dx in range(NX):
        bytes_of(blocks(NZ * NY - 1 + dx), q_recv.at[dx])
        forward_q(dx).start()
    bytes_of(kv_buf.at[0, tp, pl.ds(1, SLOTS - 1)], kv_recv.at[0])
    for copy in own_kv:
        copy.wait()
    forward_kv(0).start()
    send_kv(1)
    send_kv(2)
    forward_kv(0).wait_recv()

    ones = jnp.ones((chunk_keys, HD), jnp.bfloat16)

    def chosen(chunk, kind, query_group):
        pieces = []
        for slot in range(SLOTS):
            key_group = group_ref[chunk * SLOTS + slot]
            fresh = jnp.logical_or(
                time_ref[key_group] < time_ref[query_group], key_group == query_group
            )
            for core in range(2):
                pieces.append(
                    jnp.where(
                        fresh,
                        kv_buf[chunk, core, slot, kind, 0],
                        kv_buf[chunk, core, slot, kind, 1],
                    )
                )
        return jnp.concatenate(pieces, axis=0)

    def attend(chunk, half, dx):
        first = (half * NX + dx) * NZ
        query_pipe = (pipe + dx + half) % 2

        def score(number):
            queries = q_buf[half, dx, number].reshape(block, HD)
            keys = chosen(chunk, 0, query_pipe * GPS + number)
            return lax.dot_general(
                queries, keys, (((1,), (1,)), ((), ())), preferred_element_type=jnp.float32
            )

        scores = score(0)
        for number in range(NZ):
            later = score(number + 1) if number + 1 < NZ else None
            values = chosen(chunk, 1, query_pipe * GPS + number)
            values = jnp.concatenate([values, ones], axis=1)
            before = peak[first + number, :, :1]
            now = jnp.maximum(before, jnp.max(scores, axis=1, keepdims=True) * scaling)
            weights = jnp.exp2(scores * scaling - now).astype(jnp.bfloat16)
            factor = jnp.exp2(before - now)
            acc[first + number] = acc[first + number] * factor + jnp.dot(
                weights, values, preferred_element_type=jnp.float32
            )
            peak[first + number] = jnp.broadcast_to(now, (block, HD))
            scores = later

    def finished(index):
        total = acc[index, :, HD : HD + 1]
        level = peak[index, :, :1] + jnp.log2(total)
        return acc[index, :, :HD] / total, level

    def exchange(dx):
        return (
            remote(part_out.at[dx], part_in.at[dx], part_send.at[dx], part_recv.at[dx], across),
            remote(lse_out.at[dx], lse_in.at[dx], lse_send.at[dx], lse_recv.at[dx], across),
        )

    def hand_over(dx):
        lane = lax.broadcasted_iota(jnp.int32, (block, HD), 1)
        levels = jnp.zeros((block, HD), jnp.float32)
        for number in range(NZ):
            mixed, level = finished((NX + dx) * NZ + number)
            part_out[dx, number] = mixed.astype(jnp.bfloat16)
            remote(
                part_out.at[dx, number], part_in.at[dx, number],
                part_send.at[dx], part_recv.at[dx], across,
            ).start()
            levels = jnp.where(lane == number, level, levels)
        wide = jnp.concatenate(
            [levels, jnp.zeros((lse_out.shape[2] - block, HD), jnp.float32)], axis=0
        )
        lse_out[dx] = jnp.transpose(wide)[:8]
        remote(
            lse_out.at[dx], lse_in.at[dx], lse_send.at[dx], lse_recv.at[dx], across
        ).start()

    def give_back(dx):
        for copy in exchange(dx):
            copy.wait_recv()
        other_levels = jnp.transpose(jnp.concatenate([lse_in[dx]] * (HD // 8), axis=0))[:block]
        for number in range(NZ):
            mine, level = finished(dx * NZ + number)
            other_level = other_levels[:, number : number + 1]
            top = jnp.maximum(level, other_level)
            share, other_share = jnp.exp2(level - top), jnp.exp2(other_level - top)
            both = 1.0 / (share + other_share)
            mixed = mine * (share * both) + part_in[dx, number].astype(jnp.float32) * (
                other_share * both
            )
            done_buf[dx, number] = mixed.astype(jnp.bfloat16).reshape(NY, rows, HD)

            def send_back(back_y, _):
                other = (number * NY + back_y) * NX + (x + dx) % NX
                target = {"seq": other, "pipe": (pipe + dx) % 2}

                @pl.when(jnp.logical_or(other != seq, dx != 0))
                def _():
                    remote(
                        done_buf.at[dx, number, back_y], head(out_ref, seq),
                        done_send, done_recv, target,
                    ).start()

                return 0

            lax.fori_loop(0, NY, send_back, 0)

    def step(index, _):
        half, dx, chunk = (lookup(index, [entry[at] for entry in ORDER]) for at in range(3))

        for at, number in ((6, 3),):

            @pl.when(index == at)
            def _():
                send_kv(number)

        @pl.when(jnp.logical_or(index == 2, index == 3))
        def _():
            forward_q(dx).wait_recv()

        for at, number in ((3, 1), (7, 2), (9, 3)):

            @pl.when(index == at)
            def _():
                bytes_of(kv_buf.at[number, tp], kv_recv.at[number])
                forward_kv(number).start()

        for at, number in ((4, 1), (8, 2), (10, 3)):

            @pl.when(index == at)
            def _():
                forward_kv(number).wait_recv()

        attend(chunk, half, dx)

        @pl.when(jnp.logical_or(index == 10, index == 11))
        def _():
            hand_over(dx)

        @pl.when(jnp.logical_or(index == 13, index == 15))
        def _():
            give_back(dx)

        return 0

    lax.fori_loop(0, 4 * CHUNKS, step, 0)

    own_out = pltpu.make_async_copy(done_buf.at[0, z, y], head(out_ref, seq), local_sem.at[5])
    own_out.start()
    own_out.wait()
    for dx in range(NX):
        bytes_of(blocks(NZ * NY - 1 + dx), q_send.at[dx])
        forward_q(dx).wait_send()
    bytes_of(kv_buf.at[0, tp, pl.ds(1, SLOTS - 1)], kv_send.at[0])
    for chunk in range(1, CHUNKS):
        bytes_of(kv_buf.at[chunk, tp], kv_send.at[chunk])
    for chunk in range(CHUNKS):
        forward_kv(chunk).wait_send()
    for dx in range(NX):
        for copy in exchange(dx):
            copy.wait_send()
    bytes_of(blocks(CHUNKS * SLOTS - 1), done_send)
    bytes_of(blocks(CHUNKS * SLOTS - 1), done_recv)


def local(queries, keys, values, stale_keys, stale_values, group_order):
    rows, columns = queries.shape
    block = NY * rows
    dma = pltpu.SemaphoreType.DMA
    anywhere = pl.BlockSpec(memory_space=pl.ANY)
    return pl.pallas_call(
        kernel,
        out_shape=jax.ShapeDtypeStruct((rows, columns), jnp.bfloat16),
        in_specs=[pl.BlockSpec(memory_space=pltpu.SMEM)] + [anywhere] * 5,
        out_specs=anywhere,
        scratch_shapes=[
            pltpu.VMEM((2, NX, NZ, NY, rows, HD), jnp.bfloat16),
            pltpu.VMEM((CHUNKS, 2, SLOTS, 2, 2, rows, HD), jnp.bfloat16),
            pltpu.VMEM((2 * NX * NZ, block, 2 * HD), jnp.float32),
            pltpu.VMEM((2 * NX * NZ, block, HD), jnp.float32),
            pltpu.VMEM((NX, NZ, block, HD), jnp.bfloat16),
            pltpu.VMEM((NX, NZ, block, HD), jnp.bfloat16),
            pltpu.VMEM((NX, 8, 512), jnp.float32),
            pltpu.VMEM((NX, 8, 512), jnp.float32),
            pltpu.VMEM((NX, NZ, NY, rows, HD), jnp.bfloat16),
            pltpu.SMEM((2 * GPS,), jnp.int32),
            pltpu.SMEM((CHUNKS * SLOTS,), jnp.int32),
            dma((6,)), dma((NX,)), dma((NX,)), dma((NX,)), dma((NX,)),
            dma((CHUNKS,)), dma((CHUNKS,)), dma((CHUNKS,)), dma((CHUNKS,)),
            dma((NX,)), dma((NX,)), dma((NX,)), dma((NX,)), dma, dma,
        ],
        compiler_params=pltpu.CompilerParams(
            collective_id=0, has_side_effects=True, vmem_limit_bytes=60 * 2**20
        ),
    )(group_order, queries, keys, values, stale_keys, stale_values)


def solution(mesh):
    placed = P(("pipe", "seq", "tp"), None)
    return jax.shard_map(
        local, mesh=mesh, in_specs=(placed,) * 5 + (P(),), out_specs=placed, check_vma=False
    )
```
